256 devices in a mesh: seq: 64 (over z, x, core), head: 4 (over y).
Axes of the slice: x: 4, y: 4, z: 8, core: 2. Of those that a mesh axis runs over, the one named last changes fastest.
Arguments:
- queries: bfloat16 [4, 16384, 128], P('head', 'seq'), may hold values from -8 to 8
- keys: bfloat16 [4, 16384, 128], P('head', 'seq'), may hold values from -6 to 6
- state_b: bfloat16 [4, 16384, 128], P('head', 'seq'), may hold values from -6 to 6
- state_c: bfloat16 [4, 16384, 128], P('head', 'seq'), may hold values from -6 to 6
- decay: float32 [4, 16384], P('head', 'seq'), may hold values from -1 to 0, as said below
Outputs:
- grad_b: float32 [4, 16384, 128], P('head', 'seq')
- grad_c: float32 [4, 16384, 128], P('head', 'seq')
- grad_decay: float32 [4, 16384], P('head', 'seq')
- distance: float32 [], replicated
The draws below stay inside these ranges and needn't reach their ends.
Inputs may be any that keep to these rules, and one draw needn't show every extreme that they name: decay is negative.
All inputs are finite; a program needn't handle non-finite values.
Results may differ from the reference program's by a relative error of at most 0.00096.
Values may be sent and summed in bfloat16 or wider, within the bound.
A program may use at most 128 MiB of HBM per device.

```python
import math
import jax
import jax.numpy as jnp
from jax import lax

DH = 128
NSTATE = 128
TOK_DEV = 256
TOKENS = 16384
HEADS = 4


def teacher_pair(key):
    base = jax.random.normal(jax.random.fold_in(key, 101), (2, HEADS, TOKENS, DH), jnp.float32)
    return base


def draw_queries(key, part):
    base = teacher_pair(key)
    values = jnp.clip(2.0 * base[0], -8.0, 8.0)
    return values.astype(jnp.bfloat16)


def draw_keys(key, part):
    base = teacher_pair(key)
    values = jnp.clip(base[1], -4.0, 4.0)
    return values.astype(jnp.bfloat16)


def draw_decay(key, part):
    key = jax.random.fold_in(key, 3)
    streams = jax.random.split(key, 6)
    order = jax.random.permutation(streams[0], HEADS)
    slow_heads = order < HEADS // 2
    slow_rate = jnp.exp(jax.random.uniform(streams[1], (HEADS,), jnp.float32, math.log(0.05), math.log(0.4))) / TOKENS
    fast_rate = jnp.exp(jax.random.uniform(streams[2], (HEADS,), jnp.float32, math.log(1.0 / 50.0), math.log(1.0 / 30.0)))
    token_rate = jnp.where(slow_heads, slow_rate, fast_rate)
    scene_scale = jnp.exp(jax.random.uniform(streams[3], (HEADS, TOKENS // TOK_DEV), jnp.float32, math.log(0.5), math.log(2.0)))
    scene_scale = jnp.repeat(scene_scale, TOK_DEV, axis=1)
    token_jitter = jax.random.uniform(streams[4], (HEADS, TOKENS), jnp.float32, 0.5, 1.5)
    third = TOKENS // 3
    reset_positions = jnp.arange(3, dtype=jnp.int32)[None, :] * third + jax.random.randint(streams[5], (HEADS, 3), 0, third)
    reset_strength = jax.random.uniform(jax.random.fold_in(key, 9), (HEADS, 3), jnp.float32, 0.2, 0.5)
    token_positions = jnp.arange(TOKENS, dtype=jnp.int32)
    reset_terms = jnp.sum(jnp.where(token_positions[None, None, :] == reset_positions[:, :, None], jnp.log(1.0 - reset_strength)[:, :, None], 0.0), axis=1)
    return -(token_rate[:, None] * scene_scale * token_jitter) + reset_terms


def block_levels(stream_key, shape, shards, least, top_value):
    factor_of = 1.0
    for position, parts in shards:
        heights = jax.random.uniform(jax.random.fold_in(jax.random.fold_in(stream_key, 6), position), (parts,), jnp.float32, least / len(shards), top_value / len(shards))
        factor_of = factor_of * jnp.repeat(jnp.exp(heights), shape[position] // parts).reshape((-1,) + (1,) * (len(shape) - 1 - position))
    return factor_of


def centred(key, dims, scale, reach, cuts=(), held_as=jnp.bfloat16):
    level = block_levels(key, dims, cuts, -0.22, 0.18) if cuts else 1.0
    array = jax.random.normal(key, dims, jnp.float32) * scale * level
    return jnp.minimum(jnp.maximum(array, -reach), reach).astype(held_as)


def setup_inputs(seed: int = 0) -> dict:
    splits = jax.random.split(jax.random.key(seed), 6)
    return {
        "queries": draw_queries(jax.random.fold_in(splits[5], 71), 0),
        "keys": draw_keys(jax.random.fold_in(splits[5], 71), 0),
        "state_b": centred(splits[2], (HEADS, TOKENS, NSTATE), 1.0, 6.0, ((0, 4), (1, 64))),
        "state_c": centred(splits[3], (HEADS, TOKENS, NSTATE), 1.0, 6.0, ((0, 4), (1, 64))),
        "decay": draw_decay(jax.random.fold_in(splits[5], 71), 0),
    }


floor_score = -1e+30

def score_block(query_rows, key_rows):
    return jnp.dot(query_rows, key_rows.T, preferred_element_type=jnp.float32) / math.sqrt(query_rows.shape[1])

def pair_block(scores, causal, log_total, cum_query, cum_key, output_rows, input_rows, weight):
    attention = jnp.where(causal, jnp.exp(scores - log_total[:, None]), 0.0)
    spread = jnp.where(causal, jnp.exp(jnp.minimum(cum_query[:, None] - cum_key[None, :], 0.0)), 0.0)
    student = weight * spread * jnp.dot(output_rows, input_rows.T, preferred_element_type=jnp.float32)
    misfit = student - attention
    return ((misfit * spread).astype(jnp.bfloat16), misfit)

def reference(queries, keys, state_b, state_c, decay):
    head_count, seq_length, head_width = queries.shape
    weight = 4.0 / TOKENS
    cum_all = jnp.cumsum(decay, axis=1)
    block_rows = math.gcd(seq_length, 1024)
    grads_in = []
    grads_out = []
    grads_decay = []
    square_sum = jnp.zeros((), jnp.float32)
    for head_index in range(head_count):
        query_head = queries[head_index]
        key_head = keys[head_index]
        input_head = state_b[head_index]
        output_head = state_c[head_index]
        cum_head = cum_all[head_index]
        grad_in = jnp.zeros((seq_length, state_b.shape[2]), jnp.float32)
        pieces_out = []
        for block_index in range(seq_length // block_rows):
            row_begin = block_index * block_rows
            row_end = row_begin + block_rows
            query_rows = query_head[row_begin:row_end]
            output_rows = output_head[row_begin:row_end]
            key_rows = key_head[:row_end]
            input_rows = input_head[:row_end]
            pos_query = jnp.arange(row_begin, row_end, dtype=jnp.int32)
            pos_key = jnp.arange(row_end, dtype=jnp.int32)
            causal = pos_query[:, None] >= pos_key[None, :]
            scores = score_block(query_rows, key_rows)
            running_max = lax.optimization_barrier(jnp.max(jnp.where(causal, scores, floor_score), axis=1))
            denominator = lax.optimization_barrier(jnp.sum(jnp.where(causal, jnp.exp(scores - running_max[:, None]), 0.0), axis=1))
            log_total = running_max + jnp.log(denominator)
            mixed_tile, misfit = pair_block(scores, causal, log_total, cum_head[row_begin:row_end], cum_head[:row_end], output_rows, input_rows, weight)
            pieces_out.append(jnp.dot(mixed_tile, input_rows, preferred_element_type=jnp.float32))
            grad_in = grad_in.at[:row_end].add(jnp.dot(mixed_tile.T, output_rows, preferred_element_type=jnp.float32))
            square_sum = square_sum + jnp.sum(misfit * misfit)
        grad_out = jnp.concatenate(pieces_out, axis=0)
        cum_gradient = lax.optimization_barrier(jnp.sum(output_head.astype(jnp.float32) * grad_out, axis=1)) - lax.optimization_barrier(jnp.sum(input_head.astype(jnp.float32) * grad_in, axis=1))
        behind = jnp.flip(jnp.cumsum(jnp.flip(cum_gradient)))
        grads_in.append(grad_in)
        grads_out.append(grad_out)
        grads_decay.append(behind / math.sqrt(TOKENS))
    distance = jnp.sqrt(square_sum / (head_count * TOKENS))
    return (jnp.stack(grads_in), jnp.stack(grads_out), jnp.stack(grads_decay), distance)
```

```python
import math

import jax
import jax.numpy as jnp
from jax import lax
from jax.experimental import pallas as pl
from jax.experimental.pallas import tpu as pltpu
from jax.sharding import PartitionSpec as P

SIDE = 8
STEPS = (1, -2, 3, 4)
UNITS = len(STEPS)
SLOTS = SIDE + UNITS
LOG2E = math.log2(math.e)
FLOOR = -1e30
F32 = jnp.float32
BF16 = jnp.bfloat16


def dot_nt(a, b):
    return lax.dot_general(a, b, (((1,), (1,)), ((), ())), preferred_element_type=F32)


def dot_nn(a, b):
    return lax.dot_general(a, b, (((1,), (0,)), ((), ())), preferred_element_type=F32)


def running(x, reverse):
    width = x.shape[-1]
    lane = lax.broadcasted_iota(jnp.int32, x.shape, x.ndim - 1)
    step = 1
    while step < width:
        if reverse:
            x = x + jnp.where(lane < width - step, pltpu.roll(x, width - step, x.ndim - 1), 0.0)
        else:
            x = x + jnp.where(lane >= step, pltpu.roll(x, step, x.ndim - 1), 0.0)
        step *= 2
    return x


def spread_lanes(column, width):
    return jnp.broadcast_to(column, (column.shape[0], width))


def kernel(
    heads, total_rows,
    q_hbm, k_hbm, b_hbm, c_hbm, dec_hbm,
    gb_out, gc_out, gd_out, dist_out,
    QK, CB, BT, DEC, GCOL, CUMCOL, E, MB, ST, RST, RSTX, LB, CUMV, REFV, D1, D2,
    GB, GCT, RGB, RGCT, RXB, RXC, SQ, T1, T2, T3,
    load_sem, qk_send, qk_recv, qkx_send, qkx_recv, cb_send, cb_recv, cbx_send, cbx_recv,
    d1_send, d1_recv, d2_send, d2_recv, st_send, st_recv, stx_send, stx_recv,
    l_send, l_recv, lx_send, lx_recv, gb_send, gb_recv, gc_send, gc_recv, gx_send, gx_recv,
    t1_send, t1_recv, t2_send, t2_recv, t3_send, t3_recv,
):
    n = lax.axis_index("seq")
    h = lax.axis_index("head")
    z = lax.div(n, SIDE)
    b = lax.rem(n, SIDE)
    R = q_hbm.shape[0]
    weight = 4.0 / total_rows
    scale2 = LOG2E / math.sqrt(q_hbm.shape[1])

    def mate(o):
        return {"seq": z * SIDE + o}

    def other(row):
        return {"seq": row * SIDE + b}

    def send(src, dst, ssem, rsem, where):
        pltpu.make_async_remote_copy(src, dst, ssem, rsem, device_id=where).start()

    def got(ref, ssem, rsem):
        pltpu.make_async_remote_copy(ref, ref, ssem, rsem, device_id=mate(b)).wait_recv()

    def sent(ref, ssem, rsem):
        pltpu.make_async_remote_copy(ref, ref, ssem, rsem, device_id=mate(b)).wait_send()

    def around(t):
        return lax.rem(b + t, SIDE)

    def row_of(u):
        return lax.rem(z + STEPS[u] + SIDE, SIDE)

    def holder(u):
        return lax.rem(z - STEPS[u] + SIDE, SIDE)

    def each_mate(body):
        def one(t, carry):
            body(lax.rem(b + t, SIDE))
            return carry

        lax.fori_loop(1, SIDE, one, 0)

    def each_row(body):
        def one(t, carry):
            body(lax.rem(z + t, SIDE))
            return carry

        lax.fori_loop(1, SIDE, one, 0)

    loads = [
        pltpu.make_async_copy(dec_hbm, DEC, load_sem.at[0]),
        pltpu.make_async_copy(q_hbm, QK.at[2 * b], load_sem.at[1]),
        pltpu.make_async_copy(k_hbm, QK.at[2 * b + 1], load_sem.at[2]),
        pltpu.make_async_copy(b_hbm, CB.at[2 * b + 1], load_sem.at[3]),
        pltpu.make_async_copy(c_hbm, CB.at[2 * b], load_sem.at[4]),
    ]
    for one in loads:
        one.start()
    barrier = pltpu.get_barrier_semaphore()
    each_mate(lambda o: pl.semaphore_signal(barrier, inc=1, device_id=mate(o)))
    each_row(lambda r: pl.semaphore_signal(barrier, inc=1, device_id=other(r)))
    for step in range(1, heads):
        pl.semaphore_signal(barrier, inc=1, device_id={"head": lax.rem(h + step, heads)})

    loads[0].wait()
    own_cum = running(DEC[...] * LOG2E, False)
    own_total = jnp.broadcast_to(own_cum[:, R - 1 : R], (1, R))
    D1[b] = jnp.broadcast_to(own_cum, (8, R))
    cum_col = jnp.broadcast_to(own_cum, (128, R)).T
    CUMCOL[...] = cum_col

    def columns(cum):
        column = jnp.broadcast_to(cum, (128, R)).T
        return jnp.exp2(jnp.minimum(column[R - 1 : R, :] - column, 0.0))

    for one in loads[1:]:
        one.wait()
    pl.semaphore_wait(barrier, 2 * (SIDE - 1) + heads - 1)

    each_mate(lambda o: send(D1.at[b], D1.at[b], d1_send.at[o], d1_recv.at[b], mate(o)))
    for u in range(UNITS):
        mine = 2 * b + jnp.where(z > holder(u), 0, 1)
        send(QK.at[mine], QK.at[2 * SIDE + u], qkx_send.at[u], qkx_recv.at[u], other(holder(u)))
    each_mate(lambda o: send(QK.at[pl.ds(2 * b, 2)], QK.at[pl.ds(2 * b, 2)], qk_send.at[o], qk_recv.at[b], mate(o)))
    for u in range(UNITS):
        mine = 2 * b + jnp.where(z > holder(u), 0, 1)
        send(CB.at[mine], CB.at[2 * SIDE + u], cbx_send.at[u], cbx_recv.at[u], other(holder(u)))
    each_mate(lambda o: send(CB.at[pl.ds(2 * b, 2)], CB.at[pl.ds(2 * b, 2)], cb_send.at[o], cb_recv.at[b], mate(o)))

    def clear(s, carry):
        GB[s] = jnp.zeros((R, 128), F32)
        GCT[s] = jnp.zeros((128, R), F32)
        ST[s, 0:1, :] = jnp.full((1, R), FLOOR, F32)
        ST[s, 1:2, :] = jnp.zeros((1, R), F32)
        return carry

    lax.fori_loop(0, SLOTS, clear, 0)
    SQ[...] = jnp.zeros_like(SQ)

    each_mate(lambda o: got(D1.at[o], d1_send.at[o], d1_recv.at[o]))
    before = jnp.zeros((1, R), F32)
    total = jnp.zeros((1, R), F32)
    starts = []
    for o in range(SIDE):
        part = jnp.broadcast_to(D1[o, 0:1, R - 1 : R], (1, R))
        starts.append(total)
        before = before + jnp.where(o < b, part, 0.0)
        total = total + part
    D2[z, 0:1, :] = own_cum
    D2[z, 1:2, :] = before
    D2[z, 2:3, :] = total
    each_row(lambda r: send(D2.at[z], D2.at[z], d2_send.at[r], d2_recv.at[z], other(r)))

    jj = lax.broadcasted_iota(jnp.int32, (R, R), 0)
    ii = lax.broadcasted_iota(jnp.int32, (R, R), 1)

    def note(s, m, l):
        old_m = ST[s, 0:1, :]
        old_l = ST[s, 1:2, :]
        new_m = jnp.maximum(old_m, m)
        ST[s, 0:1, :] = new_m
        ST[s, 1:2, :] = old_l * jnp.exp2(old_m - new_m) + l * jnp.exp2(m - new_m)

    def first(ri, ci, e, rs):
        s = dot_nt(QK[ci], QK[ri]) * scale2
        m = jnp.max(s, axis=0, keepdims=True)
        p = jnp.exp2(s - m)
        E[e] = p.astype(BF16)
        MB[e] = m
        note(rs, m, jnp.sum(p, axis=0, keepdims=True))

    own_e = UNITS * SIDE
    s = jnp.where(jj <= ii, dot_nt(QK[2 * b + 1], QK[2 * b]) * scale2, FLOOR)
    m = jnp.max(s, axis=0, keepdims=True)
    p = jnp.where(jj <= ii, jnp.exp2(s - m), 0.0)
    E[own_e] = p.astype(BF16)
    MB[own_e] = m
    note(b, m, jnp.sum(p, axis=0, keepdims=True))

    def pair(t):
        o = around(t)
        return jnp.maximum(b, o), jnp.minimum(b, o)

    def in_row(t, carry):
        o = around(t)
        got(QK.at[pl.ds(2 * o, 2)], qk_send.at[o], qk_recv.at[o])

        @pl.when(jnp.logical_or(t < SIDE // 2, jnp.logical_and(t == SIDE // 2, b < SIDE // 2)))
        def _():
            hi, lo = pair(t)
            first(2 * hi, 2 * lo + 1, own_e + t, hi)

        return carry

    lax.fori_loop(1, SIDE, in_row, 0)

    def span(u):
        if STEPS[u] * 2 == SIDE:
            return jnp.where(z < SIDE // 2, 0, 1), SIDE // 2
        return 0, SIDE

    def places(u, o):
        up = row_of(u) > z
        ri = jnp.where(up, 2 * SIDE + u, 2 * o)
        ci = jnp.where(up, 2 * o + 1, 2 * SIDE + u)
        rs = jnp.where(up, SIDE + u, o)
        cs = jnp.where(up, o, SIDE + u)
        return ri, ci, rs, cs

    group = 2
    for u in range(UNITS):
        got(QK.at[2 * SIDE + u], qkx_send.at[u], qkx_recv.at[u])
        begin, count = span(u)

        def unit_first(k, carry, u=u, begin=begin):
            for g in range(group):
                t = k * group + g
                ri, ci, rs, cs = places(u, around(begin + t))
                first(ri, ci, u * SIDE + t, rs)
            return carry

        lax.fori_loop(0, count // group, unit_first, 0)

    for u in range(UNITS):
        send(ST.at[SIDE + u], RSTX.at[u], stx_send.at[u], stx_recv.at[u], other(row_of(u)))
    each_mate(lambda o: send(ST.at[o], RST.at[b], st_send.at[o], st_recv.at[b], mate(o)))

    each_row(lambda r: got(D2.at[r], d2_send.at[r], d2_recv.at[r]))
    row_start = jnp.zeros((1, R), F32)
    row_starts = []
    for r in range(SIDE):
        row_starts.append(row_start)
        row_start = row_start + D2[r, 2:3, :]
    own_start = jnp.zeros((1, R), F32)
    for r in range(SIDE):
        own_start = jnp.where(z == r, row_starts[r], own_start)
    for o in range(SIDE):
        cum = D1[o, 0:1, :] + (starts[o] + own_start)
        CUMV[o] = cum
        REFV[o] = jnp.broadcast_to(cum[:, R - 1 : R], (1, R))
    for u in range(UNITS):
        r = row_of(u)
        start = jnp.zeros((1, R), F32)
        for k in range(SIDE):
            start = jnp.where(r == k, row_starts[k], start)
        cum = D2[r, 0:1, :] + (D2[r, 1:2, :] + start)
        CUMV[SIDE + u] = cum
        REFV[SIDE + u] = jnp.broadcast_to(cum[:, R - 1 : R], (1, R))

    def factors(o):
        GCOL[o] = columns(D1[o, 0:1, :])

    factors(b)
    each_mate(factors)
    for u in range(UNITS):
        GCOL[SIDE + u] = columns(D2[row_of(u), 0:1, :])

    BT[b] = CB[2 * b + 1].astype(F32).T.astype(BF16)

    def arrive(o):
        got(CB.at[pl.ds(2 * o, 2)], cb_send.at[o], cb_recv.at[o])
        BT[o] = CB[2 * o + 1].astype(F32).T.astype(BF16)

    each_mate(arrive)
    for u in range(UNITS):
        got(CB.at[2 * SIDE + u], cbx_send.at[u], cbx_recv.at[u])
        BT[SIDE + u] = CB[2 * SIDE + u].astype(F32).T.astype(BF16)

    def add_stats(ref, s, state):
        old_m, old_l = state
        m = ref[s, 0:1, :]
        new_m = jnp.maximum(old_m, m)
        return new_m, old_l * jnp.exp2(old_m - new_m) + ref[s, 1:2, :] * jnp.exp2(m - new_m)

    state = (ST[b, 0:1, :], ST[b, 1:2, :])
    each_mate(lambda o: got(RST.at[o], st_send.at[o], st_recv.at[o]))
    for t in range(1, SIDE):
        state = add_stats(RST, around(t), state)
    for u in range(UNITS):
        got(RSTX.at[u], stx_send.at[u], stx_recv.at[u])
        state = add_stats(RSTX, u, state)
    LB[b] = jnp.broadcast_to(state[0] + jnp.log2(state[1]), (8, R))
    for u in range(UNITS):
        send(LB.at[b], LB.at[SIDE + u], lx_send.at[u], lx_recv.at[u], other(holder(u)))
    each_mate(lambda o: send(LB.at[b], LB.at[b], l_send.at[o], l_recv.at[b], mate(o)))

    def square(x):
        y = x * x
        SQ[...] += jnp.sum(y.reshape(R // 8, 8, R), axis=0)

    def wide(column):
        return jnp.concatenate([column] * (R // 128), axis=1)

    def second(ri, ci, rs, cs, e):
        a = jnp.exp2(jnp.minimum(CUMV[rs] - REFV[cs], 0.0))
        f = jnp.exp2(MB[e] - LB[rs, 0:1, :])
        apart = wide(GCOL[cs]) * a
        misfit = dot_nt(CB[ci], CB[ri]) * (apart * weight) - E[e].astype(F32) * f
        square(misfit)
        mixed = (misfit * apart).astype(BF16)
        GB[cs] += dot_nn(mixed, CB[ri])
        GCT[rs] += dot_nn(BT[cs], mixed)

    causal = jj <= ii
    apart = jnp.exp2(jnp.minimum(own_cum - wide(CUMCOL[...]), 0.0))
    spread = jnp.where(causal, apart, 0.0)
    f = jnp.exp2(MB[own_e] - LB[b, 0:1, :])
    misfit = dot_nt(CB[2 * b + 1], CB[2 * b]) * (weight * spread) - E[own_e].astype(F32) * f
    square(misfit)
    mixed = (misfit * spread).astype(BF16)
    GB[b] += dot_nn(mixed, CB[2 * b])
    GCT[b] += dot_nn(BT[b], mixed)

    each_mate(lambda o: got(LB.at[o], l_send.at[o], l_recv.at[o]))
    for u in reversed(range(UNITS)):
        got(LB.at[SIDE + u], lx_send.at[u], lx_recv.at[u])
        begin, count = span(u)

        def unit_second(k, carry, u=u, begin=begin):
            for g in range(group):
                t = k * group + g
                ri, ci, rs, cs = places(u, around(begin + t))
                second(ri, ci, rs, cs, u * SIDE + t)
            return carry

        lax.fori_loop(0, count // group, unit_second, 0)
        up = row_of(u) > z

        @pl.when(up)
        def _(u=u):
            send(GCT.at[SIDE + u], RXC.at[u], gx_send.at[u], gx_recv.at[u], other(row_of(u)))

        @pl.when(jnp.logical_not(up))
        def _(u=u):
            send(GB.at[SIDE + u], RXB.at[u], gx_send.at[u], gx_recv.at[u], other(row_of(u)))

    def in_row_second(t, carry):
        @pl.when(jnp.logical_or(t < SIDE // 2, jnp.logical_and(t == SIDE // 2, b < SIDE // 2)))
        def _():
            hi, lo = pair(t)
            second(2 * hi, 2 * lo + 1, hi, lo, own_e + t)

        o = around(t)
        send(GB.at[o], RGB.at[b], gb_send.at[o], gb_recv.at[b], mate(o))
        send(GCT.at[o], RGCT.at[b], gc_send.at[o], gc_recv.at[b], mate(o))
        return carry

    lax.fori_loop(1, SIDE, in_row_second, 0)

    sq = jnp.sum(jnp.sum(SQ[...], axis=0, keepdims=True), axis=1, keepdims=True)
    T1[b, 1:2, :] = jnp.broadcast_to(sq, (1, R))

    for u in range(UNITS):

        @pl.when(z > holder(u))
        def _(u=u):
            got(RXC.at[u], gx_send.at[u], gx_recv.at[u])
            GCT[b] += RXC[u]

        @pl.when(z < holder(u))
        def _(u=u):
            got(RXB.at[u], gx_send.at[u], gx_recv.at[u])
            GB[b] += RXB[u]

    def add_mate(o):
        got(RGB.at[o], gb_send.at[o], gb_recv.at[o])
        GB[b] += RGB[o]
        got(RGCT.at[o], gc_send.at[o], gc_recv.at[o])
        GCT[b] += RGCT[o]

    each_mate(add_mate)
    grad_c = GCT[b].T
    grad_b = GB[b]
    gc_out[...] = grad_c
    gb_out[...] = grad_b
    flow = CB[2 * b].astype(F32) * grad_c - CB[2 * b + 1].astype(F32) * grad_b
    flow = jnp.sum(flow.T, axis=0, keepdims=True)
    behind = running(flow, True)
    T1[b, 0:1, :] = jnp.broadcast_to(behind[:, 0:1], (1, R))
    each_mate(lambda o: send(T1.at[b], T1.at[b], t1_send.at[o], t1_recv.at[b], mate(o)))
    each_mate(lambda o: got(T1.at[o], t1_send.at[o], t1_recv.at[o]))
    later = jnp.zeros((1, R), F32)
    row_flow = jnp.zeros((1, R), F32)
    row_sq = jnp.zeros((1, R), F32)
    for o in range(SIDE):
        later = later + jnp.where(o > b, T1[o, 0:1, :], 0.0)
        row_flow = row_flow + T1[o, 0:1, :]
        row_sq = row_sq + T1[o, 1:2, :]
    T2[z, 0:1, :] = row_flow
    T2[z, 1:2, :] = row_sq
    each_row(lambda r: send(T2.at[z], T2.at[z], t2_send.at[r], t2_recv.at[z], other(r)))
    each_row(lambda r: got(T2.at[r], t2_send.at[r], t2_recv.at[r]))
    head_sq = jnp.zeros((1, R), F32)
    for r in range(SIDE):
        later = later + jnp.where(r > z, T2[r, 0:1, :], 0.0)
        head_sq = head_sq + T2[r, 1:2, :]
    T3[h, 0:1, :] = head_sq
    for step in range(1, heads):
        to = lax.rem(h + step, heads)
        send(T3.at[h], T3.at[h], t3_send.at[to], t3_recv.at[h], {"head": to})
    gd_out[...] = (behind + later) * (1.0 / math.sqrt(total_rows))
    for step in range(1, heads):
        o = lax.rem(h + step, heads)
        got(T3.at[o], t3_send.at[o], t3_recv.at[o])
    everything = jnp.zeros((1, R), F32)
    for k in range(heads):
        everything = everything + T3[k, 0:1, :]
    dist_out[...] = jnp.sqrt(everything[:, :128] / (heads * total_rows))

    def drain(o):
        sent(D1.at[b], d1_send.at[o], d1_recv.at[b])
        sent(QK.at[pl.ds(2 * b, 2)], qk_send.at[o], qk_recv.at[b])
        sent(CB.at[pl.ds(2 * b, 2)], cb_send.at[o], cb_recv.at[b])
        sent(ST.at[o], st_send.at[o], st_recv.at[b])
        sent(LB.at[b], l_send.at[o], l_recv.at[b])
        sent(GB.at[o], gb_send.at[o], gb_recv.at[b])
        sent(GCT.at[o], gc_send.at[o], gc_recv.at[b])
        sent(T1.at[b], t1_send.at[o], t1_recv.at[b])

    each_mate(drain)

    def drain_row(r):
        sent(D2.at[z], d2_send.at[r], d2_recv.at[z])
        sent(T2.at[z], t2_send.at[r], t2_recv.at[z])

    each_row(drain_row)
    for step in range(1, heads):
        to = lax.rem(h + step, heads)
        sent(T3.at[h], t3_send.at[to], t3_recv.at[h])
    for u in range(UNITS):
        mine = 2 * b + jnp.where(z > holder(u), 0, 1)
        sent(QK.at[mine], qkx_send.at[u], qkx_recv.at[u])
        sent(CB.at[mine], cbx_send.at[u], cbx_recv.at[u])
        sent(ST.at[SIDE + u], stx_send.at[u], stx_recv.at[u])
        sent(LB.at[b], lx_send.at[u], lx_recv.at[u])
        up = row_of(u) > z

        @pl.when(up)
        def _(u=u):
            sent(GCT.at[SIDE + u], gx_send.at[u], gx_recv.at[u])

        @pl.when(jnp.logical_not(up))
        def _(u=u):
            sent(GB.at[SIDE + u], gx_send.at[u], gx_recv.at[u])


def local(queries, keys, state_b, state_c, decay):
    rows, width = queries.shape[1:]
    devices = lax.axis_size("seq")
    heads = lax.axis_size("head")
    total_rows = rows * devices
    assert devices == SIDE * SIDE and width == 128 and rows % 128 == 0
    blocks = UNITS * SIDE + SIDE // 2 + 1

    def vm(*shape, dtype=F32):
        return pltpu.VMEM(shape, dtype)

    def sems(*shape):
        return pltpu.SemaphoreType.DMA(shape)

    scratch = [
        vm(2 * SIDE + UNITS, rows, width, dtype=BF16),
        vm(2 * SIDE + UNITS, rows, width, dtype=BF16),
        vm(SLOTS, width, rows, dtype=BF16),
        vm(1, rows),
        vm(SLOTS, rows, width),
        vm(rows, width),
        vm(blocks, rows, rows, dtype=BF16),
        vm(blocks, 1, rows),
        vm(SLOTS, 8, rows),
        vm(SIDE, 8, rows),
        vm(UNITS, 8, rows),
        vm(SLOTS, 8, rows),
        vm(SLOTS, 1, rows),
        vm(SLOTS, 1, rows),
        vm(SIDE, 8, rows),
        vm(SIDE, 8, rows),
        vm(SLOTS, rows, width),
        vm(SLOTS, width, rows),
        vm(SIDE, rows, width),
        vm(SIDE, width, rows),
        vm(UNITS, rows, width),
        vm(UNITS, width, rows),
        vm(8, rows),
        vm(SIDE, 8, rows),
        vm(SIDE, 8, rows),
        vm(heads, 8, rows),
        sems(5),
        sems(SIDE), sems(SIDE), sems(UNITS), sems(UNITS),
        sems(SIDE), sems(SIDE), sems(UNITS), sems(UNITS),
        sems(SIDE), sems(SIDE), sems(SIDE), sems(SIDE),
        sems(SIDE), sems(SIDE), sems(UNITS), sems(UNITS),
        sems(SIDE), sems(SIDE), sems(UNITS), sems(UNITS),
        sems(SIDE), sems(SIDE), sems(SIDE), sems(SIDE), sems(UNITS), sems(UNITS),
        sems(SIDE), sems(SIDE), sems(SIDE), sems(SIDE), sems(heads), sems(heads),
    ]

    def body(*refs):
        kernel(heads, total_rows, *refs)

    anywhere = pl.BlockSpec(memory_space=pl.ANY)
    inside = pl.BlockSpec(memory_space=pltpu.VMEM)
    grad_b, grad_c, grad_decay, distance = pl.pallas_call(
        body,
        out_shape=(
            jax.ShapeDtypeStruct((rows, width), F32),
            jax.ShapeDtypeStruct((rows, width), F32),
            jax.ShapeDtypeStruct((1, rows), F32),
            jax.ShapeDtypeStruct((1, 128), F32),
        ),
        in_specs=[anywhere] * 5,
        out_specs=(inside,) * 4,
        scratch_shapes=scratch,
        compiler_params=pltpu.CompilerParams(
            collective_id=0, has_side_effects=True, vmem_limit_bytes=44 * 1024 * 1024
        ),
    )(queries[0], keys[0], state_b[0], state_c[0], decay)
    return grad_b[None], grad_c[None], grad_decay, distance[0, 0]


def solution(mesh):
    return jax.shard_map(
        local,
        mesh=mesh,
        in_specs=(
            P("head", "seq", None),
            P("head", "seq", None),
            P("head", "seq", None),
            P("head", "seq", None),
            P("head", "seq"),
        ),
        out_specs=(P("head", "seq", None), P("head", "seq", None), P("head", "seq"), P()),
        check_vma=False,
    )
```
